32 devices in a mesh: grp: 2 (over x), ep: 16 (over z, y, core).
Axes of the slice: x: 2, y: 2, z: 4, core: 2. Of those that a mesh axis runs over, the one named last changes fastest.
Arguments:
- tokens: bfloat16 [4096, 3584], P(('grp', 'ep')), parts along dimension 0, may hold values from -6 to 6
- expert_ids: int32 [4096, 8], P(('grp', 'ep')), parts along dimension 0, may hold values from 0 to 15, all different within a row
- gate_weights: float32 [4096, 8], P(('grp', 'ep')), parts along dimension 0, may hold values from 0.1 to 1
- use_copy: int32 [4096, 8], P(('grp', 'ep')), parts along dimension 0, may hold values 0 or 1
- expert_weights: bfloat16 [16, 3584, 3072], P('ep'), may hold values from -0.09375 to 0.09375
Outputs:
- mixed: bfloat16 [4096, 3584], P(('grp', 'ep')), parts along dimension 0
The draws below stay inside these ranges and needn't reach their ends.
There are 2 independent parts, one for each index of `grp`. The reference program is written for one: setup_inputs(seed, part) draws one part's arguments, and reference() takes and returns one part's arrays. A program takes and returns all parts, laid end to end along the dimension named above; an argument that names none is the same for every part. Nothing has to cross between parts.
Inputs may be any that keep to these rules, and one draw needn't show every extreme that they name: `expert_ids`: each token names 8 different experts.
All inputs are finite; a program needn't handle non-finite values. No bound on the sum of `use_copy` on one device may be relied on, other than what follows from the above.
Results may differ from the reference program's by a relative error of at most 0.0059.
Values may be sent and summed in bfloat16 or wider, within the bound.
A program may use at most 192 MiB of HBM per device.

```python
import jax
import jax.numpy as jnp
from jax import lax

D = 3584
F = 1024
TOP = 8
TOK_DEV = 128
EXPERTS = 16
TOKENS = 2048
CAP = 40
N_EP = 16


def set_ends(values, own_key, smallest, high):
    extent = values.shape
    spot = [jax.random.randint(jax.random.fold_in(own_key, axis), (), 0, extent[axis]) for axis in range(len(extent))]
    values = values.at[tuple(spot)].set(smallest)
    longest = extent.index(max(extent))
    spot[longest] = (spot[longest] + 1) % extent[longest]
    return values.at[tuple(spot)].set(high)


def shard_levels(rng, shape, pieces, smallest, high):
    factor_of = 1.0
    for position, shards_of in pieces:
        heights = jax.random.uniform(jax.random.fold_in(jax.random.fold_in(rng, 6), position), (shards_of,), jnp.float32, smallest / len(pieces), high / len(pieces))
        factor_of = factor_of * jnp.repeat(jnp.exp(heights), shape[position] // shards_of).reshape((-1,) + (1,) * (len(shape) - 1 - position))
    return factor_of


def distinct(stream_key, rows, number_of, top, lift):
    order = jax.random.permutation(jax.random.fold_in(stream_key, 1), number_of)
    favour = order
    for power in range(3):
        favour = favour * favour // number_of
    favour = favour * lift // number_of
    lots = jax.random.randint(jax.random.fold_in(stream_key, 2), (rows, number_of), 0, 4096) + favour
    sure = jax.random.permutation(jax.random.fold_in(stream_key, 3), rows)[jnp.arange(number_of) % rows]
    lots = jnp.where(jnp.arange(rows)[:, None] == sure[None, :], 1 << 14, lots)
    priority = lots * number_of + jnp.arange(number_of)
    return lax.top_k(priority.astype(jnp.int32), top)[1].astype(jnp.int32)


def gaussian(rng, dims, deviation, most, shards=(), held_as=jnp.bfloat16):
    entries = deviation * jax.random.normal(rng, dims, jnp.float32)
    if shards:
        entries = entries * shard_levels(rng, dims, shards, -0.22, 0.18)
    return jnp.clip(entries, -most, most).astype(held_as)


def setup_inputs(seed: int = 0, part: int = 0) -> dict:
    streams_of = jax.random.split(jax.random.key(seed), 6)
    part_splits = jax.random.split(jax.random.fold_in(streams_of[5], part), 6)
    return {
        "tokens": gaussian(part_splits[0], (TOKENS, D), 1.0, 6.0, ((0, 16),)),
        "expert_ids": distinct(part_splits[1], TOKENS, EXPERTS, TOP, 8192),
        "gate_weights": jnp.clip(0.1 + 0.9 * jax.random.uniform(part_splits[2], (TOKENS, TOP), jnp.float32) ** shard_levels(part_splits[2], (TOKENS, TOP), ((0, 16),), -0.2, 0.2), 0.1, 1.0),
        "use_copy": set_ends((jax.random.randint(part_splits[3], (TOKENS, TOP), 0, 2) < 1).astype(jnp.int32), jax.random.fold_in(part_splits[3], 1), 0, 1),
        "expert_weights": gaussian(streams_of[4], (EXPERTS, D, 3 * F), D ** -0.5, 0.09375, ((0, 16),)),
    }


def expert_rows(rows, weights):
    width = weights.shape[1] // 3
    both = jnp.dot(rows, weights[:, :2 * width], preferred_element_type=jnp.float32)
    hidden = (jax.nn.silu(both[:, :width]) * both[:, width:]).astype(jnp.bfloat16)
    output = lax.dot_general(hidden, weights[:, 2 * width:], (((1,), (1,)), ((), ())), preferred_element_type=jnp.float32)
    return output.astype(jnp.bfloat16)


def reference(tokens, expert_ids, gate_weights, use_copy, expert_weights):
    half = N_EP // 2
    target = jnp.bitwise_xor(expert_ids, use_copy * half).reshape(N_EP, TOK_DEV * TOP)
    copy_flag = use_copy.reshape(N_EP, TOK_DEV * TOP)
    bucket = target * 2 + copy_flag
    onehot = (bucket[:, :, None] == jnp.arange(2 * N_EP, dtype=jnp.int32)[None, None, :]).astype(jnp.int32)
    before = jnp.sum((jnp.cumsum(onehot, axis=1) - onehot) * onehot, axis=2)
    kept = before < CAP
    source = jnp.arange(N_EP, dtype=jnp.int32)[:, None]
    slots = N_EP * N_EP * CAP * 2
    place = jnp.where(kept, ((target * N_EP + source) * CAP + before) * 2 + copy_flag, slots).reshape(-1)
    copies = jnp.repeat(tokens, TOP, axis=0)
    buffer = jnp.zeros((slots, D), jnp.bfloat16).at[place].set(copies, mode="drop").reshape(N_EP, N_EP * CAP, 2, D)

    def serve(inputs):
        rank, rows = inputs
        first = expert_rows(rows[:, 0, :], expert_weights[rank])
        second = expert_rows(rows[:, 1, :], expert_weights[jnp.bitwise_xor(rank, half)])
        return jnp.stack([first, second], axis=1)

    results = lax.map(serve, (jnp.arange(N_EP, dtype=jnp.int32), buffer)).reshape(slots, D)
    picked = jnp.take(results, jnp.minimum(place, slots - 1), axis=0).reshape(TOKENS, TOP, D)
    weight = jnp.where(kept.reshape(TOKENS, TOP), gate_weights, jnp.float32(0.0))
    total = jnp.zeros((TOKENS, D), jnp.float32)
    for choice_index in range(TOP):
        total = total + picked[:, choice_index, :].astype(jnp.float32) * weight[:, choice_index:choice_index + 1]
    return total.astype(jnp.bfloat16)
```

```python
import jax
import jax.numpy as jnp
from jax import lax
from jax.sharding import PartitionSpec as P

CHUNKS = 2


def routing(expert_ids, gate_weights, use_copy, ranks):
    half = ranks // 2
    tok_rows, top_count = expert_ids.shape
    capacity = tok_rows * top_count * 5 // (8 * ranks)
    lanes = jnp.arange(ranks, dtype=jnp.int32)
    hit = expert_ids[:, :, None] == lanes[None, None, :]
    home = jnp.sum(jnp.where(hit & (use_copy[:, :, None] == 0), 1, 0), axis=1)
    away = jnp.sum(jnp.where(hit & (use_copy[:, :, None] == 1), 1, 0), axis=1)
    counts = jnp.concatenate([home, away], axis=1).astype(jnp.bfloat16)
    rows = jnp.arange(tok_rows, dtype=jnp.int32)
    earlier = (rows[:, None] > rows[None, :]).astype(jnp.bfloat16)
    before = jnp.dot(earlier, counts, preferred_element_type=jnp.float32)
    kept = jnp.where(before < capacity, counts.astype(jnp.float32), 0.0)
    kept = kept[:, :ranks] + kept[:, ranks:]
    weight = jnp.sum(jnp.where(hit, gate_weights[:, :, None], 0.0), axis=1)
    return weight * kept


def per_device(tokens, expert_ids, gate_weights, use_copy, expert_weights):
    ranks = lax.axis_size("ep")
    tok_rows, model_width = tokens.shape
    weights = expert_weights[0]
    width = weights.shape[1] // 3
    table = routing(expert_ids, gate_weights, use_copy, ranks)
    mine = lax.all_to_all(table.T, "ep", split_axis=0, concat_axis=0, tiled=True)
    step = tok_rows // CHUNKS
    outs = []
    for index in range(CHUNKS):
        part = tokens[index * step : (index + 1) * step]
        rows = lax.all_gather(part, "ep", axis=0, tiled=True)
        both = jnp.dot(rows, weights[:, : 2 * width], preferred_element_type=jnp.float32)
        hidden = (jax.nn.silu(both[:, :width]) * both[:, width:]).astype(jnp.bfloat16)
        output = lax.dot_general(
            hidden,
            weights[:, 2 * width :],
            (((1,), (1,)), ((), ())),
            preferred_element_type=jnp.float32,
        )
        scale = mine[:, index * step : (index + 1) * step].reshape(-1, 1)
        output = (output * scale).astype(jnp.bfloat16)
        outs.append(lax.psum_scatter(output, "ep", scatter_dimension=0, tiled=True))
    return jnp.concatenate(outs, axis=0)


def solution(mesh):
    placed = (
        P(("grp", "ep"), None),
        P(("grp", "ep"), None),
        P(("grp", "ep"), None),
        P(("grp", "ep"), None),
        P("ep", None, None),
    )
    return jax.shard_map(
        per_device, mesh=mesh, in_specs=placed, out_specs=P(("grp", "ep"), None), check_vma=False
    )
```

```python
import jax
import jax.numpy as jnp
from jax import lax
from jax.sharding import PartitionSpec as P

CHUNKS = 4


def routing(expert_ids, gate_weights, use_copy, ranks):
    half = ranks // 2
    tok_rows, top_count = expert_ids.shape
    capacity = tok_rows * top_count * 5 // (8 * ranks)
    lanes = jnp.arange(ranks, dtype=jnp.int32)
    hit = expert_ids[:, :, None] == lanes[None, None, :]
    home = jnp.sum(jnp.where(hit & (use_copy[:, :, None] == 0), 1, 0), axis=1)
    away = jnp.sum(jnp.where(hit & (use_copy[:, :, None] == 1), 1, 0), axis=1)
    counts = jnp.concatenate([home, away], axis=1).astype(jnp.bfloat16)
    rows = jnp.arange(tok_rows, dtype=jnp.int32)
    earlier = (rows[:, None] > rows[None, :]).astype(jnp.bfloat16)
    before = jnp.dot(earlier, counts, preferred_element_type=jnp.float32)
    kept = jnp.where(before < capacity, counts.astype(jnp.float32), 0.0)
    kept = kept[:, :ranks] + kept[:, ranks:]
    weight = jnp.sum(jnp.where(hit, gate_weights[:, :, None], 0.0), axis=1)
    return weight * kept


def swap(value, bit):
    ranks = lax.axis_size("ep")
    return lax.ppermute(value, "ep", [(i, i ^ bit) for i in range(ranks)])


def expert_rows(rows, weights, scale):
    width = weights.shape[1] // 3
    both = jnp.dot(rows, weights[:, : 2 * width], preferred_element_type=jnp.float32)
    hidden = (jax.nn.silu(both[:, :width]) * both[:, width:]).astype(jnp.bfloat16)
    output = lax.dot_general(
        hidden,
        weights[:, 2 * width :],
        (((1,), (1,)), ((), ())),
        preferred_element_type=jnp.float32,
    )
    return output * scale


def per_device(tokens, expert_ids, gate_weights, use_copy, expert_weights):
    ranks = lax.axis_size("ep")
    me = lax.axis_index("ep")
    tok_rows, model_width = tokens.shape
    weights = expert_weights[0]
    order = [1 << b for b in reversed(range(ranks.bit_length() - 1))]
    stages = len(order)
    table = routing(expert_ids, gate_weights, use_copy, ranks).T[None]
    step = tok_rows // CHUNKS
    state = [tokens[index * step : (index + 1) * step] for index in range(CHUNKS)]
    for slot in range(CHUNKS + 2 * stages):
        fresh = list(state)
        for index in range(CHUNKS):
            stage = slot - index
            value = state[index]
            if 0 <= stage < stages:
                fresh[index] = (value, swap(value, order[stage]))
            elif stage == stages:
                scale = lax.dynamic_index_in_dim(table, me, axis=1, keepdims=False)
                scale = scale[:, index * step : (index + 1) * step].reshape(-1, 1)
                fresh[index] = expert_rows(value, weights, scale).astype(jnp.bfloat16)
            elif stages < stage <= 2 * stages:
                size = value.shape[0] // 2
                other = swap(value[size:], order[2 * stages - stage])
                fresh[index] = (value[:size], other)
        if slot < stages:
            table_next = (table, swap(table, order[slot]))
        else:
            table_next = table
        fresh, table_next = lax.optimization_barrier((fresh, table_next))
        for index in range(CHUNKS):
            stage = slot - index
            if 0 <= stage < stages:
                fresh[index] = jnp.concatenate(fresh[index], axis=0)
            elif stages < stage <= 2 * stages:
                kept, other = fresh[index]
                total = kept.astype(jnp.float32) + other.astype(jnp.float32)
                fresh[index] = total.astype(jnp.bfloat16)
        state = fresh
        table = jnp.concatenate(table_next, axis=0) if slot < stages else table_next
    return jnp.concatenate(state, axis=0)


def solution(mesh):
    placed = (
        P(("grp", "ep"), None),
        P(("grp", "ep"), None),
        P(("grp", "ep"), None),
        P(("grp", "ep"), None),
        P("ep", None, None),
    )
    return jax.shard_map(
        per_device, mesh=mesh, in_specs=placed, out_specs=P(("grp", "ep"), None), check_vma=False
    )
```

```python
import jax
import jax.numpy as jnp
from jax import lax
from jax.sharding import PartitionSpec as P

CHUNKS = 4


def routing(expert_ids, gate_weights, use_copy, ranks):
    half = ranks // 2
    tok_rows, top_count = expert_ids.shape
    capacity = tok_rows * top_count * 5 // (8 * ranks)
    lanes = jnp.arange(ranks, dtype=jnp.int32)
    hit = expert_ids[:, :, None] == lanes[None, None, :]
    home = jnp.sum(jnp.where(hit & (use_copy[:, :, None] == 0), 1, 0), axis=1)
    away = jnp.sum(jnp.where(hit & (use_copy[:, :, None] == 1), 1, 0), axis=1)
    counts = jnp.concatenate([home, away], axis=1).astype(jnp.bfloat16)
    rows = jnp.arange(tok_rows, dtype=jnp.int32)
    earlier = (rows[:, None] > rows[None, :]).astype(jnp.bfloat16)
    before = jnp.dot(earlier, counts, preferred_element_type=jnp.float32)
    kept = jnp.where(before < capacity, counts.astype(jnp.float32), 0.0)
    kept = kept[:, :ranks] + kept[:, ranks:]
    weight = jnp.sum(jnp.where(hit, gate_weights[:, :, None], 0.0), axis=1)
    return weight * kept


def swap(value, bit):
    ranks = lax.axis_size("ep")
    return lax.ppermute(value, "ep", [(i, i ^ bit) for i in range(ranks)])


def expert_rows(rows, weights, scale):
    width = weights.shape[1] // 3
    both = jnp.dot(rows, weights[:, : 2 * width], preferred_element_type=jnp.float32)
    hidden = (jax.nn.silu(both[:, :width]) * both[:, width:]).astype(jnp.bfloat16)
    output = lax.dot_general(
        hidden,
        weights[:, 2 * width :],
        (((1,), (1,)), ((), ())),
        preferred_element_type=jnp.float32,
    )
    return output * scale


def per_device(tokens, expert_ids, gate_weights, use_copy, expert_weights):
    ranks = lax.axis_size("ep")
    me = lax.axis_index("ep")
    tok_rows, model_width = tokens.shape
    weights = expert_weights[0]
    order = [1 << b for b in reversed(range(1, ranks.bit_length() - 1))]
    back = [order[-2], order[-1]] + order[:-2][::-1]
    stages = len(order)
    table = routing(expert_ids, gate_weights, use_copy, ranks).T[None]
    step = tok_rows // CHUNKS
    state = [tokens[index * step : (index + 1) * step] for index in range(CHUNKS)]

    def join(pair):
        return jnp.concatenate(pair, axis=0)

    def add(pair):
        kept, other = pair
        return (kept.astype(jnp.float32) + other.astype(jnp.float32)).astype(jnp.bfloat16)

    def halves(value, bit):
        size = value.shape[0] // 2
        return (value[:size], swap(value[size:], bit))

    for slot in range(CHUNKS + 2 * stages):
        into, out = slot - stages, slot - stages - 1
        opens = False
        if 0 <= into < CHUNKS:
            state[into] = (state[into], swap(state[into], 1))
            opens = True
        if 0 <= out < CHUNKS:
            state[out] = halves(state[out], 1)
            opens = True
        if slot == stages:
            table = (table, swap(table, 1))
        if opens:
            state, table = lax.optimization_barrier((state, table))
        if 0 <= into < CHUNKS:
            state[into] = join(state[into])
        if 0 <= out < CHUNKS:
            state[out] = add(state[out])
        if slot == stages:
            table = lax.dynamic_index_in_dim(join(table), me, axis=1, keepdims=False)
        fresh = list(state)
        for index in range(CHUNKS):
            stage = slot - index
            value = state[index]
            if 0 <= stage < stages:
                fresh[index] = (value, swap(value, order[stage]))
            elif stage == stages:
                scale = table[:, index * step : (index + 1) * step].reshape(-1, 1)
                fresh[index] = expert_rows(value, weights, scale).astype(jnp.bfloat16)
            elif stages < stage <= 2 * stages:
                bit = back[stage - stages - 1]
                if stage == stages + 1:
                    quarters = value.reshape(2, 2, -1, model_width)
                    rows = value.shape[0] // 2
                    sent = quarters[:, 1].reshape(rows, model_width)
                    kept = quarters[:, 0].reshape(rows, model_width)
                    fresh[index] = (kept, swap(sent, bit))
                else:
                    fresh[index] = halves(value, bit)
        if slot < stages:
            table = (table, swap(table, order[slot]))
        fresh, table = lax.optimization_barrier((fresh, table))
        for index in range(CHUNKS):
            stage = slot - index
            if 0 <= stage < stages:
                fresh[index] = join(fresh[index])
            elif stages < stage <= 2 * stages:
                fresh[index] = add(fresh[index])
        if slot < stages:
            table = join(table)
        state = list(fresh)
    return jnp.concatenate(state, axis=0)


def solution(mesh):
    placed = (
        P(("grp", "ep"), None),
        P(("grp", "ep"), None),
        P(("grp", "ep"), None),
        P(("grp", "ep"), None),
        P("ep", None, None),
    )
    return jax.shard_map(
        per_device, mesh=mesh, in_specs=placed, out_specs=P(("grp", "ep"), None), check_vma=False
    )
```
